128 devices in a mesh: shot: 4 (over z), slab: 32 (over y, x, core).
Axes of the slice: x: 4, y: 4, z: 4, core: 2. Of those that a mesh axis runs over, the one named last changes fastest.
Arguments:
- courant: float32 [4, 256, 256, 256], P('shot', 'slab'), may hold values from 0.05 to 0.3
- adj_prev: float32 [4, 256, 256, 256], P('shot', 'slab'), may hold values from -6 to 6
- adj_cur: float32 [4, 256, 256, 256], P('shot', 'slab'), may hold values from -6 to 6
- accel: float32 [4, 3, 256, 256, 256], P('shot', None, 'slab'), may hold values from -6 to 6
- res_data: float32 [4, 3, 512], P('shot'), may hold values from -6 to 6
- rec_index: int32 [4, 512], P('shot'), may hold values from 0 to 16777215
- intersection: int32 [4, 8], P('shot'), may hold values from 0 to 15, as said below
- model: float32 [256, 512, 256], P('slab', 'shot'), may hold values from 0.5 to 2
Outputs:
- new_model: float32 [256, 512, 256], P('slab', 'shot')
- adj_state: float32 [4, 256, 256, 256], P('shot', 'slab')
- born_field: float32 [4, 256, 256, 256], P('shot', 'slab')
The draws below stay inside these ranges and needn't reach their ends.
Inputs may be any that keep to these rules, and one draw needn't show every extreme that they name: `intersection`: each shot's ids are 8 consecutive tiles; some shot starts at 0 and some shot ends at 15.
All inputs are finite; a program needn't handle non-finite values.
Results may differ from the reference program's by a relative error of at most 0.00012.
Values sent between devices are 32-bit elements; how exact they have to be, the bound alone decides.
A program may use at most 128 MiB of HBM per device.

```python
import jax
import jax.numpy as jnp

AX = 256
AY = 256
TX = 32
NREC = 512
NZ = 256
SHOTS = 4
LT = 8
MLAT = 16
MX = 512


def draw_intersection(key, part):
    key = jax.random.fold_in(key, 11)
    first_key, second_key = jax.random.split(key)
    starts = jax.random.randint(first_key, (SHOTS,), 0, MLAT - LT + 1)
    order = jax.random.permutation(second_key, SHOTS)
    starts = starts.at[order[0]].set(0).at[order[1]].set(MLAT - LT)
    return (starts[:, None] + jnp.arange(LT)[None, :]).astype(jnp.int32)


def set_ends(array, stream_key, low, largest):
    dims = array.shape
    index_at = [jax.random.randint(jax.random.fold_in(stream_key, axis), (), 0, dims[axis]) for axis in range(len(dims))]
    array = array.at[tuple(index_at)].set(low)
    longest = dims.index(max(dims))
    index_at[longest] = (index_at[longest] + 1) % dims[longest]
    return array.at[tuple(index_at)].set(largest)


def block_levels(rng, dims, shards, smallest, high):
    loudness = 1.0
    for axis_at, shards_of in shards:
        steps = jax.random.uniform(jax.random.fold_in(jax.random.fold_in(rng, 6), axis_at), (shards_of,), jnp.float32, smallest / len(shards), high / len(shards))
        loudness = loudness * jnp.repeat(jnp.exp(steps), dims[axis_at] // shards_of).reshape((-1,) + (1,) * (len(dims) - 1 - axis_at))
    return loudness


def gaussian(key, dims, deviation, limit, cuts=(), held_as=jnp.bfloat16):
    result = jax.random.normal(key, dims, jnp.float32) * deviation
    if len(cuts) > 0:
        result = block_levels(key, dims, cuts, -0.22, 0.18) * result
    return jnp.clip(result, min=-limit, max=limit).astype(held_as)


def setup_inputs(seed: int = 0) -> dict:
    arg_keys = jax.random.split(jax.random.key(seed), 9)
    courant = jnp.clip(0.05 + 0.25 * jax.random.uniform(arg_keys[0], (SHOTS, NZ, AX, AY), jnp.float32) ** block_levels(arg_keys[0], (SHOTS, NZ, AX, AY), ((0, 4), (1, 32)), -0.2, 0.2), 0.05, 0.3)
    adj_prev = gaussian(arg_keys[1], (SHOTS, NZ, AX, AY), 1.0, 6.0, ((0, 4), (1, 32)), jnp.float32)
    adj_cur = gaussian(arg_keys[2], (SHOTS, NZ, AX, AY), 1.0, 6.0, ((0, 4), (1, 32)), jnp.float32)
    accel = gaussian(arg_keys[3], (SHOTS, 3, NZ, AX, AY), 1.0, 6.0, ((0, 4), (2, 32)), jnp.float32)
    res_data = gaussian(arg_keys[4], (SHOTS, 3, NREC), 1.0, 6.0, ((0, 4),), jnp.float32)
    rec_index = set_ends(jax.random.randint(arg_keys[5], (SHOTS, NREC), 0, NZ * AX * AY), jax.random.fold_in(arg_keys[5], 1), 0, (NZ * AX * AY) - 1).astype(jnp.int32)
    intersection = draw_intersection(jax.random.fold_in(arg_keys[8], 71), 0)
    model = jnp.clip(0.5 + 1.5 * jax.random.uniform(arg_keys[7], (NZ, MX, AY), jnp.float32) ** block_levels(arg_keys[7], (NZ, MX, AY), ((0, 32), (1, 4)), -0.2, 0.2), 0.5, 2.0)
    return {"courant": courant, "adj_prev": adj_prev, "adj_cur": adj_cur, "accel": accel, "res_data": res_data, "rec_index": rec_index, "intersection": intersection, "model": model}


def lap_inner(ext):
    center = ext[1:-1]
    side = jnp.pad(center, ((0, 0), (1, 1), (1, 1)))
    nbrs = ext[:-2] + ext[2:] + side[:, :-2, 1:-1] + side[:, 2:, 1:-1] + side[:, 1:-1, :-2] + side[:, 1:-1, 2:]
    return nbrs - 6.0 * center


def wave_step(ext, before, coeff):
    return 2.0 * ext[1:-1] - before + coeff * lap_inner(ext)


def padded(field):
    return jnp.pad(field, ((1, 1), (0, 0), (0, 0)))


def inject(field, receivers, values):
    shape = field.shape
    return field.reshape(-1).at[receivers].add(values).reshape(shape)


def sample(field, receivers):
    return field.reshape(-1)[receivers]


def reference(courant, adj_prev, adj_cur, accel, res_data, rec_index, intersection, model):
    grad = jnp.zeros((NZ, MLAT, TX, AY), jnp.float32)
    states = []
    for shot_id in range(SHOTS):
        coeff = courant[shot_id]
        first = inject(wave_step(padded(adj_cur[shot_id]), adj_prev[shot_id], coeff), rec_index[shot_id], res_data[shot_id, 2])
        second = inject(wave_step(padded(first), adj_cur[shot_id], coeff), rec_index[shot_id], res_data[shot_id, 1])
        image = accel[shot_id, 1] * first + accel[shot_id, 0] * second
        grad = grad.at[:, intersection[shot_id]].add(image.reshape(NZ, LT, TX, AY))
        states.append(second)
    num = jnp.zeros((), jnp.float32)
    den = jnp.zeros((), jnp.float32)
    borns = []
    for shot_id in range(SHOTS):
        coeff = courant[shot_id]
        gap = grad[:, intersection[shot_id]].reshape(NZ, AX, AY)
        weight = coeff * gap
        before = jnp.zeros((NZ, AX, AY), jnp.float32)
        now = jnp.zeros((NZ, AX, AY), jnp.float32)
        for tick in range(3):
            later = wave_step(padded(now), before, coeff) + weight * accel[shot_id, tick]
            trace = sample(later, rec_index[shot_id])
            num = num + jnp.sum(res_data[shot_id, tick] * trace)
            den = den + jnp.sum(trace * trace)
            before, now = now, later
        borns.append(now)
    alpha = num / (den + 1e-6)
    new_model = model - alpha * grad.reshape(NZ, MX, AY)
    return new_model, jnp.stack(states), jnp.stack(borns)
```

```python
import functools

import jax
import jax.numpy as jnp
from jax import lax
from jax.experimental import pallas as pl
from jax.experimental.pallas import tpu as pltpu
from jax.sharding import PartitionSpec as P

MESH = pl.DeviceIdType.MESH
ORDER = (1, 2, 0, 3, 7, 4, 6, 5)
FIRST = (0, 1, 6, 7)


def radices(count):
    out = []
    while count > 1:
        step = 4 if count % 4 == 0 and (out or count == 4) else 2
        out.append(step)
        count //= step
    return out


def kernel(
    dims,
    inter_ref, res_ref, rec_ref, courant, prev, cur, accel, model,
    nm_out, adj_out, born_out,
    ac, ach, co, ap, ax, mo, p1, p1h, ad, img, v1, s2, w2, part,
    qd, ct, b1, b1h, b2, b2h, b3, wt, exs, exr, own, nm, stv, ar,
    ld, outs, h_s, h_r, p_s, p_r, b_s, b_r, st_s, st_r, z1_s, z1_r, z2_s, z2_r, ex_s, ex_r, ar_s, ar_r,
):
    shots, slabs, depth, wide, width, tiles, tx, nrec = dims
    f32 = jnp.float32
    z = lax.axis_index("shot")
    k = lax.axis_index("slab")
    par = z % 2
    pair_a = z + 1 - 2 * par
    pair_b = shots - 1 - z
    up = (k + 1) % slabs
    down = (k + slabs - 1) % slabs

    phases = []
    stride = 1
    for n in radices(slabs):
        coord = (k // stride) % n
        base = k - coord * stride
        phases.append((n, coord, [(z, base + ((coord + d) % n) * stride) for d in range(1, n)]))
        stride *= n
    phases.append((shots, z, [((z + d) % shots, k) for d in range(1, shots)]))

    barrier = pltpu.get_barrier_semaphore()
    greet = [(z, up), (z, down)] + [dev for phase in phases for dev in phase[2]]
    for dev in greet:
        pl.semaphore_signal(barrier, inc=1, device_id=dev, device_id_type=MESH)

    def strip(j):
        return slice(j * tx, j * tx + tx)

    def load(src, dst, at):
        copies = [pltpu.make_async_copy(src.at[:, strip(j)], dst.at[j], ld.at[at, j]) for j in range(tiles)]
        for copy in copies:
            copy.start()
        return copies

    l_cur = load(cur.at[0], ac, 0)
    l_co = load(courant.at[0], co, 1)
    l_ap = load(prev.at[0], ap, 2)
    l_a1 = load(accel.at[0, 1], ax.at[1], 3)
    l_a0 = load(accel.at[0, 0], ax.at[0], 4)
    l_a2 = load(accel.at[0, 2], ax.at[2], 5)
    l_mo = pltpu.make_async_copy(model, mo, ld.at[6, 0])
    l_mo.start()

    def wait(copies):
        for copy in copies:
            copy.wait()

    def remote(src, dst, send, recv, dev):
        return pltpu.make_async_remote_copy(
            src_ref=src, dst_ref=dst, send_sem=send, recv_sem=recv, device_id=dev, device_id_type=MESH
        )

    start = inter_ref[0, 0]
    stv[0] = jnp.full(stv.shape[1:], start, jnp.int32)

    pl.semaphore_wait(barrier, len(greet))

    halos_c = []
    for j in range(tiles):
        halos_c.append(remote(cur.at[0, depth - 1, strip(j)], ach.at[0, j], h_s.at[0, j], h_r.at[0, j], (z, up)))
        halos_c.append(remote(cur.at[0, 0, strip(j)], ach.at[1, j], h_s.at[1, j], h_r.at[1, j], (z, down)))
    for copy in halos_c:
        copy.start()
    st_a = remote(stv.at[0], stv.at[1], st_s.at[0], st_r.at[0], (pair_a, k))
    st_b = remote(stv.at[0], stv.at[2], st_s.at[1], st_r.at[1], (pair_b, k))
    st_a.start()
    st_b.start()

    rec = rec_ref[...] - k * (depth * wide * width)
    inside = (rec >= 0) & (rec < depth * wide * width)
    line = rec // width
    down_at, along = line // wide, line % wide
    row = jnp.where(inside, (along // tx * depth + down_at) * tx + along % tx, -1)
    col = rec % width
    col_at = lax.broadcasted_iota(jnp.int32, (width, nrec), 0) == col
    for f in range(4):
        rest = res_ref[0, f : f + 1, :] if f < 3 else jnp.ones((1, nrec), f32)
        for piece in range(3 if f < 3 else 1):
            bits = rest.astype(jnp.bfloat16).astype(f32)
            rest = rest - bits
            ct[3 * f + piece] = jnp.where(col_at, bits, 0.0).astype(jnp.bfloat16)

    def receivers(fields):
        def plane(d, carry):
            at = lax.broadcasted_iota(jnp.int32, (depth * tx, nrec), 0) + d * (depth * tx)
            hot = jnp.where(at == row, 1.0, 0.0).astype(jnp.bfloat16)
            for f in fields:
                total = None
                for piece in range(3 if f < 3 else 1):
                    term = lax.dot_general(
                        hot, ct[3 * f + piece], (((1,), (1,)), ((), ())), preferred_element_type=f32
                    )
                    total = term if total is None else total + term
                for i in range(depth):
                    qd[f, d, i] = total[i * tx : i * tx + tx]
            return carry

        lax.fori_loop(0, tiles, plane, 0)

    receivers((2, 1))

    lane = lax.broadcasted_iota(jnp.int32, (tx, width), 1)

    def lap(c, below, above, before, after):
        big = jnp.concatenate([before, c, after], axis=0)
        n = below + above
        n = n + pltpu.roll(big, 1, 0)[8 : tx + 8]
        n = n + pltpu.roll(big, tx + 15, 0)[8 : tx + 8]
        n = n + jnp.where(lane == 0, 0.0, pltpu.roll(c, 1, 1))
        n = n + jnp.where(lane == width - 1, 0.0, pltpu.roll(c, width - 1, 1))
        return n - 6.0 * c

    def cells(field, halos, d, i, j):
        c = field[i, d]
        before = jnp.where(j == 0, 0.0, field[(i + tiles - 1) % tiles, d, tx - 8 : tx])
        after = jnp.where(j == tiles - 1, 0.0, field[(i + 1) % tiles, d, 0:8])
        edge_low = isinstance(d, int) and d == 0
        edge_high = isinstance(d, int) and d == depth - 1
        below = jnp.where(k == 0, 0.0, halos[0, i]) if edge_low else field[i, d - 1]
        above = jnp.where(k == slabs - 1, 0.0, halos[1, i]) if edge_high else field[i, d + 1]
        return c, lap(c, below, above, before, after)

    def interior(body):
        def plane(d, carry):
            def one(j, inner):
                body(d, j)
                return inner

            return lax.fori_loop(0, tiles, one, carry, unroll=2)

        lax.fori_loop(1, depth - 1, plane, 0)

    def p1_cell(d, j):
        c, l = cells(ac, ach, d, j, j)
        p1[j, d] = 2.0 * c - ap[j, d] + co[j, d] * l + qd[2, j, d]

    def p1_sends(j):
        return (
            remote(p1.at[j, depth - 1], p1h.at[0, j], p_s.at[0, j], p_r.at[0, j], (z, up)),
            remote(p1.at[j, 0], p1h.at[1, j], p_s.at[1, j], p_r.at[1, j], (z, down)),
        )

    wait(l_cur)
    wait(l_co)
    wait(l_ap)
    interior(p1_cell)
    for copy in halos_c:
        copy.wait_recv()

    def p1_edge(j, carry):
        p1_cell(0, j)
        p1_cell(depth - 1, j)
        for copy in p1_sends(j):
            copy.start()
        return carry

    lax.fori_loop(0, tiles, p1_edge, 0)

    def ad_cell(d, j):
        c, l = cells(p1, p1h, d, j, j)
        ad[j, d] = 2.0 * c - ac[j, d] + co[j, d] * l + qd[1, j, d]

    interior(ad_cell)

    def ad_edge(j, carry):
        for copy in p1_sends(j):
            copy.wait_recv()
        ad_cell(0, j)
        ad_cell(depth - 1, j)
        return carry

    lax.fori_loop(0, tiles, ad_edge, 0)
    o_ad = [pltpu.make_async_copy(ad.at[j], adj_out.at[0, :, strip(j)], outs.at[0, j]) for j in range(tiles)]
    for copy in o_ad:
        copy.start()

    wait(l_a1)
    wait(l_a0)
    wait(l_a2)

    def place(r):
        return (r - start) & (tiles - 1)

    def send1(r):
        dev = (pair_a if r in FIRST else pair_b, k)
        return remote(img.at[r], v1.at[r], z1_s.at[r], z1_r.at[r], dev)

    def send2(r):
        dev = (pair_b if r in FIRST else pair_a, k)
        return remote(s2.at[r], w2.at[r], z2_s.at[r], z2_r.at[r], dev)

    for r in ORDER:
        at = place(r)

        def image(d, carry, r=r, at=at):
            img[r, d] = ax[1, at, d] * p1[at, d] + ax[0, at, d] * ad[at, d]
            return carry

        lax.fori_loop(0, depth, image, 0, unroll=True)
        send1(r).start()

    receivers((0, 3))
    st_a.wait_recv()
    st_b.wait_recv()

    def group(slot, r):
        cell = jnp.where(stv[slot] > r, 1, 0)
        across = jnp.concatenate([cell] * (width // 128), axis=1)
        return jnp.concatenate([across] * (tx // 8), axis=0)

    for r in ORDER:
        first, second = (1, 2) if r in FIRST else (2, 1)
        send1(r).wait_recv()
        g_own, g_src, g_dst = group(0, r), group(first, r), group(second, r)
        own_dst = g_own == g_dst
        src_dst = g_src == g_dst
        src_own = g_src == g_own

        def combine(d, carry, r=r, own_dst=own_dst, src_dst=src_dst, src_own=src_own):
            mine = img[r, d]
            theirs = v1[r, d]
            s2[r, d] = jnp.where(own_dst, mine, 0.0) + jnp.where(src_dst, theirs, 0.0)
            part[r, d] = mine + jnp.where(src_own, theirs, 0.0)
            return carry

        lax.fori_loop(0, depth, combine, 0, unroll=True)
        send2(r).start()

    half = tiles // 2

    def extra(e):
        if e < half // 2:
            dest = (1 - par) * pair_a + par * pair_b
        else:
            dest = par * pair_a + (1 - par) * pair_b
        return remote(exs.at[e], exr.at[e], ex_s.at[e], ex_r.at[e], (dest, k)), dest

    def source(r, e_low):
        return r, e_low

    for e in range(half):
        copy, dest = extra(e)
        low = e < half // 2
        r_send = (1 - par) * half + e
        r_own = par * half + e
        src_send = jnp.where((par == 1) if low else (par == 0), group(1, r_send), group(2, r_send))
        src_own = jnp.where((par == 0) if low else (par == 1), group(1, r_own), group(2, r_own))
        want_send = dest // 2
        want_own = z // 2
        m_send = group(0, r_send) == want_send
        t_send = src_send == want_send
        m_own = group(0, r_own) == want_own
        t_own = src_own == want_own

        def spread(d, carry, e=e, r_send=r_send, r_own=r_own, m_send=m_send, t_send=t_send, m_own=m_own, t_own=t_own):
            exs[e, d] = jnp.where(m_send, img[r_send, d], 0.0) + jnp.where(t_send, v1[r_send, d], 0.0)
            own[e, d] = jnp.where(m_own, img[r_own, d], 0.0) + jnp.where(t_own, v1[r_own, d], 0.0)
            return carry

        lax.fori_loop(0, depth, spread, 0, unroll=2)
        copy.start()

    def fold(m):
        m = sum(m[:, 128 * i : 128 * i + 128] for i in range(width // 128))
        return sum(m[8 * i : 8 * i + 8] for i in range(tx // 8))

    def tally(carry, t, d, at, b):
        num, den = carry
        return num + fold(qd[t, at, d] * b), den + fold(qd[3, at, d] * b * b)

    def halo_sends(level, field, halos, r):
        return (
            remote(field.at[r, depth - 1], halos.at[0, r], b_s.at[level, 0, r], b_r.at[level, 0, r], (z, up)),
            remote(field.at[r, 0], halos.at[1, r], b_s.at[level, 1, r], b_r.at[level, 1, r], (z, down)),
        )

    zero = jnp.zeros((8, 128), f32)
    sums = (zero, zero)
    for r in ORDER:
        send2(r).wait_recv()
        at = place(r)

        def born1(d, carry, r=r, at=at):
            w = co[at, d] * (part[r, d] + w2[r, d])
            wt[r, d] = w
            b = w * ax[0, at, d]
            b1[r, d] = b
            return tally(carry, 0, d, at, b)

        sums = lax.fori_loop(0, depth, born1, sums, unroll=2)
        for copy in halo_sends(0, b1, b1h, r):
            copy.start()

    def b2_cell(d, r, carry):
        j = place(r)
        c, l = cells(b1, b1h, d, r, j)
        b = 2.0 * c + co[j, d] * l + wt[r, d] * ax[1, j, d]
        b2[r, d] = b
        return tally(carry, 1, d, j, b)

    def b3_cell(d, j, carry):
        r = (j + start) & (tiles - 1)
        c, l = cells(b2, b2h, d, r, j)
        b = 2.0 * c - b1[r, d] + co[j, d] * l + wt[r, d] * ax[2, j, d]
        b3[j, d] = b
        return tally(carry, 2, d, j, b)

    def sweep(cell, carry):
        def plane(d, inner):
            return lax.fori_loop(0, tiles, lambda r, deep: cell(d, r, deep), inner, unroll=2)

        return lax.fori_loop(1, depth - 1, plane, carry)

    sums = sweep(b2_cell, sums)

    def b2_edge(r, carry):
        for copy in halo_sends(0, b1, b1h, r):
            copy.wait_recv()
        carry = b2_cell(0, r, carry)
        carry = b2_cell(depth - 1, r, carry)
        for copy in halo_sends(1, b2, b2h, r):
            copy.start()
        return carry

    sums = lax.fori_loop(0, tiles, b2_edge, sums)
    sums = sweep(b3_cell, sums)

    def b2_wait(r, carry):
        for copy in halo_sends(1, b2, b2h, r):
            copy.wait_recv()
        return carry

    lax.fori_loop(0, tiles, b2_wait, 0)

    def b3_edge(j, carry):
        carry = b3_cell(0, j, carry)
        return b3_cell(depth - 1, j, carry)

    sums = lax.fori_loop(0, tiles, b3_edge, sums)
    o_born = [pltpu.make_async_copy(b3.at[j], born_out.at[0, :, strip(j)], outs.at[1, j]) for j in range(tiles)]
    for copy in o_born:
        copy.start()

    num, den = sums
    for at, (n, coord, partners) in enumerate(phases):
        ar[at, coord, 0] = num
        ar[at, coord, 1] = den
        for d, dev in enumerate(partners):
            remote(ar.at[at, coord], ar.at[at, coord], ar_s.at[at, d], ar_r.at[at, coord], dev).start()
        for d, dev in enumerate(partners):
            other = (coord + 1 + d) % n
            remote(ar.at[at, other], ar.at[at, other], ar_s.at[at, d], ar_r.at[at, other], dev).wait_recv()
        num = ar[at, 0, 0]
        den = ar[at, 0, 1]
        for slot in range(1, n):
            num = num + ar[at, slot, 0]
            den = den + ar[at, slot, 1]
    num = jnp.sum(jnp.sum(num, axis=1, keepdims=True), axis=0, keepdims=True)
    den = jnp.sum(jnp.sum(den, axis=1, keepdims=True), axis=0, keepdims=True)
    alpha = num / (den + 1e-6)

    l_mo.wait()
    for e in range(half):
        extra(e)[0].wait_recv()

        def update(d, carry, e=e):
            cells = slice(e * tx, e * tx + tx)
            nm[d, cells, :] = mo[d, cells, :] - alpha * (own[e, d] + exr[e, d])
            return carry

        lax.fori_loop(0, depth, update, 0, unroll=2)
    o_nm = pltpu.make_async_copy(nm, nm_out, outs.at[2, 0])
    o_nm.start()

    for copy in halos_c:
        copy.wait_send()
    st_a.wait_send()
    st_b.wait_send()

    def drain(j, carry):
        for copy in p1_sends(j):
            copy.wait_send()
        for copy in halo_sends(0, b1, b1h, j):
            copy.wait_send()
        for copy in halo_sends(1, b2, b2h, j):
            copy.wait_send()
        return carry

    lax.fori_loop(0, tiles, drain, 0)
    for r in range(tiles):
        send1(r).wait_send()
        send2(r).wait_send()
    for e in range(half):
        extra(e)[0].wait_send()
    for at, (n, coord, partners) in enumerate(phases):
        for d, dev in enumerate(partners):
            remote(ar.at[at, coord], ar.at[at, coord], ar_s.at[at, d], ar_r.at[at, coord], dev).wait_send()
    wait(o_ad)
    wait(o_born)
    o_nm.wait()


def local(courant, adj_prev, adj_cur, accel, res_data, rec_index, intersection, model):
    shots, slabs = lax.axis_size("shot"), lax.axis_size("slab")
    depth, wide, width = courant.shape[1:]
    tiles = intersection.shape[1]
    tx = wide // tiles
    nrec = rec_index.shape[1]
    f32 = jnp.float32
    dims = (shots, slabs, depth, wide, width, tiles, tx, nrec)
    tiled = (tiles, depth, tx, width)
    part = (tiles // 2, depth, tx, width)
    nph = len(radices(slabs)) + 1
    dma = pltpu.SemaphoreType.DMA
    vm = pltpu.VMEM
    scratch = [
        vm(tiled, f32), vm((2, tiles, tx, width), f32), vm(tiled, f32), vm(tiled, f32), vm((3,) + tiled, f32),
        vm(model.shape, f32), vm(tiled, f32), vm((2, tiles, tx, width), f32), vm(tiled, f32),
        vm(tiled, f32), vm(tiled, f32), vm(tiled, f32), vm(tiled, f32), vm(tiled, f32),
        vm((4,) + tiled, f32), vm((10, width, nrec), jnp.bfloat16),
        vm(tiled, f32), vm((2, tiles, tx, width), f32), vm(tiled, f32), vm((2, tiles, tx, width), f32), vm(tiled, f32),
        vm(tiled, f32), vm(part, f32), vm(part, f32), vm(part, f32), vm(model.shape, f32),
        vm((3, 8, 128), jnp.int32), vm((nph, 4, 2, 8, 128), f32),
        dma((7, tiles)), dma((3, tiles)), dma((2, tiles)), dma((2, tiles)), dma((2, tiles)), dma((2, tiles)),
        dma((2, 2, tiles)), dma((2, 2, tiles)), dma((2,)), dma((2,)),
        dma((tiles,)), dma((tiles,)), dma((tiles,)), dma((tiles,)),
        dma((tiles // 2,)), dma((tiles // 2,)), dma((nph, 4)), dma((nph, 4)),
    ]
    any_spec = pl.BlockSpec(memory_space=pl.ANY)
    vm_spec = pl.BlockSpec(memory_space=pltpu.VMEM)
    return pl.pallas_call(
        functools.partial(kernel, dims),
        out_shape=(
            jax.ShapeDtypeStruct(model.shape, f32),
            jax.ShapeDtypeStruct(courant.shape, f32),
            jax.ShapeDtypeStruct(courant.shape, f32),
        ),
        in_specs=[pl.BlockSpec(memory_space=pltpu.SMEM), vm_spec, vm_spec] + [any_spec] * 5,
        out_specs=(any_spec,) * 3,
        scratch_shapes=scratch,
        compiler_params=pltpu.CompilerParams(
            collective_id=0, has_side_effects=True, vmem_limit_bytes=60 * 1024 * 1024
        ),
    )(intersection, res_data, rec_index, courant, adj_prev, adj_cur, accel, model)


def solution(mesh):
    in_specs = (
        P("shot", "slab", None, None),
        P("shot", "slab", None, None),
        P("shot", "slab", None, None),
        P("shot", None, "slab", None, None),
        P("shot", None, None),
        P("shot", None),
        P("shot", None),
        P("slab", "shot", None),
    )
    out_specs = (
        P("slab", "shot", None),
        P("shot", "slab", None, None),
        P("shot", "slab", None, None),
    )
    return jax.shard_map(local, mesh=mesh, in_specs=in_specs, out_specs=out_specs, check_vma=False)
```

```python
import functools

import jax
import jax.numpy as jnp
from jax import lax
from jax.experimental import pallas as pl
from jax.experimental.pallas import tpu as pltpu
from jax.sharding import PartitionSpec as P

MESH = pl.DeviceIdType.MESH
ORDER = (1, 2, 0, 3, 7, 4, 6, 5)
FIRST = (0, 1, 6, 7)


def kernel(
    dims,
    inter_ref, res_ref, rec_ref, courant, prev, cur, accel, model,
    nm, adj, born,
    ac, ach, co, ap, ax, mo, p1, p1h, ad, img, v1, s2, w2, part,
    qd, ct, b1, b1h, b2, b2h, wt, exs, exr, own, stv, ar,
    ld, h_s, h_r, p_s, p_r, b_s, b_r, st_s, st_r, z1_s, z1_r, z2_s, z2_r, ex_s, ex_r, ar_s, ar_r,
):
    shots, slabs, depth, wide, width, tiles, tx, nrec = dims
    f32 = jnp.float32
    z = lax.axis_index("shot")
    k = lax.axis_index("slab")
    par = z % 2
    pair_a = z + 1 - 2 * par
    pair_b = shots - 1 - z
    up = (k + 1) % slabs
    down = (k + slabs - 1) % slabs

    core = k % 2
    chip = k // 2
    chips = slabs // 2
    phases = (
        (chips, chip, [(z, (chip + d) % chips * 2 + core) for d in range(1, chips)]),
        (
            2 * shots,
            2 * z + core,
            [((2 * z + core + d) % (2 * shots) // 2, chip * 2 + (core + d) % 2) for d in range(1, 2 * shots)],
        ),
    )
    middle = list(range(2, depth - 2))
    outer = [0, 1, depth - 2, depth - 1]
    parts = (slice(0, depth - 4), slice(depth - 4, depth))
    slots = (list(enumerate(middle)), [(depth - 4 + i, d) for i, d in enumerate(outer)])

    barrier = pltpu.get_barrier_semaphore()
    greet = [(z, up), (z, down)] + [dev for phase in phases for dev in phase[2]]
    for dev in greet:
        pl.semaphore_signal(barrier, inc=1, device_id=dev, device_id_type=MESH)

    def strip(j):
        return slice(j * tx, j * tx + tx)

    def load(src, dst, at):
        copies = [pltpu.make_async_copy(src.at[:, strip(j)], dst.at[j], ld.at[at, j]) for j in range(tiles)]
        for copy in copies:
            copy.start()
        return copies

    l_cur = load(cur.at[0], ac, 0)
    l_co = load(courant.at[0], co, 1)
    l_ap = load(prev.at[0], ap, 2)
    l_a1 = load(accel.at[0, 1], ax.at[1], 3)
    l_a0 = load(accel.at[0, 0], ax.at[0], 4)
    l_a2 = load(accel.at[0, 2], ax.at[2], 5)
    l_mo = pltpu.make_async_copy(model, mo, ld.at[6, 0])
    l_mo.start()

    def wait(copies):
        for copy in copies:
            copy.wait()

    def remote(src, dst, send, recv, dev):
        return pltpu.make_async_remote_copy(
            src_ref=src, dst_ref=dst, send_sem=send, recv_sem=recv, device_id=dev, device_id_type=MESH
        )

    start = inter_ref[0, 0]
    stv[0] = jnp.full(stv.shape[1:], start, jnp.int32)

    pl.semaphore_wait(barrier, len(greet))

    halos_c = []
    for j in range(tiles):
        halos_c.append(remote(cur.at[0, depth - 1, strip(j)], ach.at[0, j], h_s.at[0, j], h_r.at[0, j], (z, up)))
        halos_c.append(remote(cur.at[0, 0, strip(j)], ach.at[1, j], h_s.at[1, j], h_r.at[1, j], (z, down)))
    for copy in halos_c:
        copy.start()
    st_a = remote(stv.at[0], stv.at[1], st_s.at[0], st_r.at[0], (pair_a, k))
    st_b = remote(stv.at[0], stv.at[2], st_s.at[1], st_r.at[1], (pair_b, k))
    st_a.start()
    st_b.start()

    rec = rec_ref[...] - k * (depth * wide * width)
    inside = (rec >= 0) & (rec < depth * wide * width)
    line = rec // width
    down_at, along = line // wide, line % wide
    row = jnp.where(inside, (along // tx * depth + down_at) * tx + along % tx, -1)
    col = rec % width
    col_at = lax.broadcasted_iota(jnp.int32, (width, nrec), 0) == col
    for f in range(4):
        rest = jnp.concatenate([res_ref[f, i : i + 1, :] for i in range(nrec // 128)], axis=1) if f < 3 else jnp.ones((1, nrec), f32)
        for piece in range(3 if f < 3 else 1):
            bits = rest.astype(jnp.bfloat16).astype(f32)
            rest = rest - bits
            ct[3 * f + piece] = jnp.where(col_at, bits, 0.0).astype(jnp.bfloat16)

    def receivers(fields):
        def plane(d, carry):
            at = lax.broadcasted_iota(jnp.int32, (depth * tx, nrec), 0) + d * (depth * tx)
            hot = jnp.where(at == row, 1.0, 0.0).astype(jnp.bfloat16)
            for f in fields:
                total = None
                for piece in range(3 if f < 3 else 1):
                    term = lax.dot_general(
                        hot, ct[3 * f + piece], (((1,), (1,)), ((), ())), preferred_element_type=f32
                    )
                    total = term if total is None else total + term
                for i in range(depth):
                    qd[f, d, i] = total[i * tx : i * tx + tx]
            return carry

        lax.fori_loop(0, tiles, plane, 0)

    receivers((2, 1))

    lane = lax.broadcasted_iota(jnp.int32, (tx, width), 1)

    def lap(c, below, above, before, after):
        big = jnp.concatenate([before, c, after], axis=0)
        n = below + above
        n = n + pltpu.roll(big, 1, 0)[8 : tx + 8]
        n = n + pltpu.roll(big, tx + 15, 0)[8 : tx + 8]
        n = n + jnp.where(lane == 0, 0.0, pltpu.roll(c, 1, 1))
        n = n + jnp.where(lane == width - 1, 0.0, pltpu.roll(c, width - 1, 1))
        return n - 6.0 * c

    def cells(field, halos, d, i, j):
        c = field[i, d]
        before = jnp.where(j == 0, 0.0, field[(i + tiles - 1) % tiles, d, tx - 8 : tx])
        after = jnp.where(j == tiles - 1, 0.0, field[(i + 1) % tiles, d, 0:8])
        edge_low = isinstance(d, int) and d == 0
        edge_high = isinstance(d, int) and d == depth - 1
        below = jnp.where(k == 0, 0.0, halos[0, i]) if edge_low else field[i, d - 1]
        above = jnp.where(k == slabs - 1, 0.0, halos[1, i]) if edge_high else field[i, d + 1]
        return c, lap(c, below, above, before, after)

    def planes(body, first, last):
        def plane(d, carry):
            def one(j, inner):
                body(d, j)
                return inner

            return lax.fori_loop(0, tiles, one, carry, unroll=2)

        lax.fori_loop(first, last, plane, 0)

    def p1_cell(d, j):
        c, l = cells(ac, ach, d, j, j)
        p1[j, d] = 2.0 * c - ap[j, d] + co[j, d] * l + qd[2, j, d]

    def p1_sends(j):
        return (
            remote(p1.at[j, depth - 1], p1h.at[0, j], p_s.at[0, j], p_r.at[0, j], (z, up)),
            remote(p1.at[j, 0], p1h.at[1, j], p_s.at[1, j], p_r.at[1, j], (z, down)),
        )

    def ad_cell(d, j):
        c, l = cells(p1, p1h, d, j, j)
        a = 2.0 * c - ac[j, d] + co[j, d] * l + qd[1, j, d]
        ad[j, d] = a
        adj[0, d, pl.ds(pl.multiple_of(j * tx, tx), tx), :] = a

    def place(r):
        return (r - start) & (tiles - 1)

    def send1(r, h):
        dev = (pair_a if r in FIRST else pair_b, k)
        return remote(img.at[r, parts[h]], v1.at[r, parts[h]], z1_s.at[r, h], z1_r.at[r, h], dev)

    def send2(r, h):
        dev = (pair_b if r in FIRST else pair_a, k)
        return remote(s2.at[r, parts[h]], w2.at[r, parts[h]], z2_s.at[r, h], z2_r.at[r, h], dev)

    def images(h):
        for r in ORDER:
            at = place(r)
            for slot, d in slots[h]:
                img[r, slot] = ax[1, at, d] * p1[at, d] + ax[0, at, d] * ad[at, d]
            send1(r, h).start()

    wait(l_cur)
    wait(l_co)
    wait(l_ap)
    planes(p1_cell, 1, depth - 1)
    planes(ad_cell, 2, depth - 2)
    wait(l_a1)
    wait(l_a0)
    wait(l_a2)
    images(0)
    for copy in halos_c:
        copy.wait_recv()

    def p1_edge(j, carry):
        p1_cell(0, j)
        p1_cell(depth - 1, j)
        for copy in p1_sends(j):
            copy.start()
        return carry

    lax.fori_loop(0, tiles, p1_edge, 0)
    planes(ad_cell, 1, 2)
    planes(ad_cell, depth - 2, depth - 1)

    def ad_edge(j, carry):
        for copy in p1_sends(j):
            copy.wait_recv()
        ad_cell(0, j)
        ad_cell(depth - 1, j)
        return carry

    lax.fori_loop(0, tiles, ad_edge, 0)
    images(1)

    receivers((0, 3))
    st_a.wait_recv()
    st_b.wait_recv()

    def group(slot, r):
        cell = jnp.where(stv[slot] > r, 1, 0)
        across = jnp.concatenate([cell] * (width // 128), axis=1)
        return jnp.concatenate([across] * (tx // 8), axis=0)

    for h in range(2):
        for r in ORDER:
            first, second = (1, 2) if r in FIRST else (2, 1)
            send1(r, h).wait_recv()
            g_own, g_src, g_dst = group(0, r), group(first, r), group(second, r)
            own_dst = g_own == g_dst
            src_dst = g_src == g_dst
            src_own = g_src == g_own
            for slot, _ in slots[h]:
                mine = img[r, slot]
                theirs = v1[r, slot]
                s2[r, slot] = jnp.where(own_dst, mine, 0.0) + jnp.where(src_dst, theirs, 0.0)
                part[r, slot] = mine + jnp.where(src_own, theirs, 0.0)
            if h == 1:
                send2(r, 1).start()
    for r in ORDER:
        send2(r, 0).start()

    half = tiles // 2

    def extra(e):
        if e < half // 2:
            dest = (1 - par) * pair_a + par * pair_b
        else:
            dest = par * pair_a + (1 - par) * pair_b
        return remote(exs.at[e], exr.at[e], ex_s.at[e], ex_r.at[e], (dest, k)), dest

    for e in range(half):
        copy, dest = extra(e)
        low = e < half // 2
        r_send = (1 - par) * half + e
        r_own = par * half + e
        src_send = jnp.where((par == 1) if low else (par == 0), group(1, r_send), group(2, r_send))
        src_own = jnp.where((par == 0) if low else (par == 1), group(1, r_own), group(2, r_own))
        want_send = dest // 2
        want_own = z // 2
        m_send = group(0, r_send) == want_send
        t_send = src_send == want_send
        m_own = group(0, r_own) == want_own
        t_own = src_own == want_own

        def spread(d, carry, e=e, r_send=r_send, r_own=r_own, m_send=m_send, t_send=t_send, m_own=m_own, t_own=t_own):
            exs[e, d] = jnp.where(m_send, img[r_send, d], 0.0) + jnp.where(t_send, v1[r_send, d], 0.0)
            own[e, d] = jnp.where(m_own, img[r_own, d], 0.0) + jnp.where(t_own, v1[r_own, d], 0.0)
            return carry

        lax.fori_loop(0, depth, spread, 0, unroll=2)
        copy.start()

    def fold(m):
        m = sum(m[:, 128 * i : 128 * i + 128] for i in range(width // 128))
        return sum(m[8 * i : 8 * i + 8] for i in range(tx // 8))

    def tally(carry, t, d, at, b):
        num, den = carry
        return num + fold(qd[t, at, d] * b), den + fold(qd[3, at, d] * b * b)

    def halo_sends(level, field, halos, r):
        return (
            remote(field.at[r, depth - 1], halos.at[0, r], b_s.at[level, 0, r], b_r.at[level, 0, r], (z, up)),
            remote(field.at[r, 0], halos.at[1, r], b_s.at[level, 1, r], b_r.at[level, 1, r], (z, down)),
        )

    zero = jnp.zeros((8, 128), f32)
    sums = (zero, zero)

    def born1(h, carry):
        for r in ORDER:
            send2(r, h).wait_recv()
            at = place(r)
            for slot, d in slots[h]:
                w = co[at, d] * (part[r, slot] + w2[r, slot])
                wt[r, d] = w
                b = w * ax[0, at, d]
                b1[r, d] = b
                carry = tally(carry, 0, d, at, b)
            if h == 1:
                for copy in halo_sends(0, b1, b1h, r):
                    copy.start()
        return carry

    sums = born1(1, sums)

    def b2_cell(d, r, carry):
        j = place(r)
        c, l = cells(b1, b1h, d, r, j)
        b = 2.0 * c + co[j, d] * l + wt[r, d] * ax[1, j, d]
        b2[r, d] = b
        return tally(carry, 1, d, j, b)

    def b3_cell(d, j, carry):
        r = (j + start) & (tiles - 1)
        c, l = cells(b2, b2h, d, r, j)
        b = 2.0 * c - b1[r, d] + co[j, d] * l + wt[r, d] * ax[2, j, d]
        born[0, d, pl.ds(pl.multiple_of(j * tx, tx), tx), :] = b
        return tally(carry, 2, d, j, b)

    def sweep(cell, carry):
        def plane(d, inner):
            return lax.fori_loop(0, tiles, lambda r, deep: cell(d, r, deep), inner, unroll=2)

        return lax.fori_loop(1, depth - 1, plane, carry)

    def b2_edge(r, carry):
        for copy in halo_sends(0, b1, b1h, r):
            copy.wait_recv()
        carry = b2_cell(0, r, carry)
        carry = b2_cell(depth - 1, r, carry)
        for copy in halo_sends(1, b2, b2h, r):
            copy.start()
        return carry

    sums = lax.fori_loop(0, tiles, b2_edge, sums)
    sums = born1(0, sums)
    sums = sweep(b2_cell, sums)
    sums = sweep(b3_cell, sums)

    def b2_wait(r, carry):
        for copy in halo_sends(1, b2, b2h, r):
            copy.wait_recv()
        return carry

    lax.fori_loop(0, tiles, b2_wait, 0)

    def b3_edge(j, carry):
        carry = b3_cell(0, j, carry)
        return b3_cell(depth - 1, j, carry)

    sums = lax.fori_loop(0, tiles, b3_edge, sums)

    row_at = lax.broadcasted_iota(jnp.int32, (8, 128), 0)
    num = jnp.sum(sums[0], axis=0, keepdims=True)
    den = jnp.sum(sums[1], axis=0, keepdims=True)
    total = jnp.where(row_at == 0, num, jnp.where(row_at == 1, den, 0.0))
    for at, (n, coord, partners) in enumerate(phases):
        ar[at, coord] = total
        for d, dev in enumerate(partners):
            remote(ar.at[at, coord], ar.at[at, coord], ar_s.at[at, d], ar_r.at[at, coord], dev).start()
        for d, dev in enumerate(partners):
            other = (coord + 1 + d) % n
            remote(ar.at[at, other], ar.at[at, other], ar_s.at[at, d], ar_r.at[at, other], dev).wait_recv()
        total = ar[at, 0]
        for slot in range(1, n):
            total = total + ar[at, slot]
    num = jnp.sum(total[0:1], axis=1, keepdims=True)
    den = jnp.sum(total[1:2], axis=1, keepdims=True)
    alpha = num / (den + 1e-6)

    l_mo.wait()
    for e in range(half):
        extra(e)[0].wait_recv()

        for slot, d in slots[0] + slots[1]:
            cells_at = slice(e * tx, e * tx + tx)
            nm[d, cells_at, :] = mo[d, cells_at, :] - alpha * (own[e, slot] + exr[e, slot])

    for copy in halos_c:
        copy.wait_send()
    st_a.wait_send()
    st_b.wait_send()

    def drain(j, carry):
        for copy in p1_sends(j):
            copy.wait_send()
        for copy in halo_sends(0, b1, b1h, j):
            copy.wait_send()
        for copy in halo_sends(1, b2, b2h, j):
            copy.wait_send()
        return carry

    lax.fori_loop(0, tiles, drain, 0)
    for r in range(tiles):
        for h in range(2):
            send1(r, h).wait_send()
            send2(r, h).wait_send()
    for e in range(half):
        extra(e)[0].wait_send()
    for at, (n, coord, partners) in enumerate(phases):
        for d, dev in enumerate(partners):
            remote(ar.at[at, coord], ar.at[at, coord], ar_s.at[at, d], ar_r.at[at, coord], dev).wait_send()

def local(courant, adj_prev, adj_cur, accel, res_data, rec_index, intersection, model):
    shots, slabs = lax.axis_size("shot"), lax.axis_size("slab")
    depth, wide, width = courant.shape[1:]
    tiles = intersection.shape[1]
    tx = wide // tiles
    nrec = rec_index.shape[1]
    f32 = jnp.float32
    dims = (shots, slabs, depth, wide, width, tiles, tx, nrec)
    tiled = (tiles, depth, tx, width)
    part = (tiles // 2, depth, tx, width)
    most = max(slabs // 2, 2 * shots)
    dma = pltpu.SemaphoreType.DMA
    vm = pltpu.VMEM
    halo = (2, tiles, tx, width)
    scratch = [
        vm(tiled, f32), vm(halo, f32), vm(tiled, f32), vm(tiled, f32), vm((3,) + tiled, f32),
        vm(model.shape, f32), vm(tiled, f32), vm(halo, f32), vm(tiled, f32),
        vm(tiled, f32), vm(tiled, f32), vm(tiled, f32), vm(tiled, f32), vm(tiled, f32),
        vm((4,) + tiled, f32), vm((10, width, nrec), jnp.bfloat16),
        vm(tiled, f32), vm(halo, f32), vm(tiled, f32), vm(halo, f32),
        vm(tiled, f32), vm(part, f32), vm(part, f32), vm(part, f32),
        vm((3, 8, 128), jnp.int32), vm((2, most, 8, 128), f32),
        dma((7, tiles)), dma((2, tiles)), dma((2, tiles)), dma((2, tiles)), dma((2, tiles)),
        dma((2, 2, tiles)), dma((2, 2, tiles)), dma((2,)), dma((2,)),
        dma((tiles, 2)), dma((tiles, 2)), dma((tiles, 2)), dma((tiles, 2)),
        dma((tiles // 2,)), dma((tiles // 2,)), dma((2, most)), dma((2, most)),
    ]
    any_spec = pl.BlockSpec(memory_space=pl.ANY)
    vm_spec = pl.BlockSpec(memory_space=pltpu.VMEM)
    return pl.pallas_call(
        functools.partial(kernel, dims),
        out_shape=(
            pltpu.VMEM(model.shape, f32),
            pltpu.VMEM(courant.shape, f32),
            pltpu.VMEM(courant.shape, f32),
        ),
        in_specs=[pl.BlockSpec(memory_space=pltpu.SMEM), vm_spec, vm_spec] + [any_spec] * 5,
        out_specs=(vm_spec,) * 3,
        scratch_shapes=scratch,
        compiler_params=pltpu.CompilerParams(
            collective_id=0, has_side_effects=True, vmem_limit_bytes=56 * 1024 * 1024
        ),
    )(intersection, res_data.reshape(3, nrec // 128, 128), rec_index, courant, adj_prev, adj_cur, accel, model)


def solution(mesh):
    in_specs = (
        P("shot", "slab", None, None),
        P("shot", "slab", None, None),
        P("shot", "slab", None, None),
        P("shot", None, "slab", None, None),
        P("shot", None, None),
        P("shot", None),
        P("shot", None),
        P("slab", "shot", None),
    )
    out_specs = (
        P("slab", "shot", None),
        P("shot", "slab", None, None),
        P("shot", "slab", None, None),
    )
    return jax.shard_map(local, mesh=mesh, in_specs=in_specs, out_specs=out_specs, check_vma=False)
```

```python
import functools

import jax
import jax.numpy as jnp
from jax import lax
from jax.experimental import pallas as pl
from jax.experimental.pallas import tpu as pltpu
from jax.sharding import PartitionSpec as P

MESH = pl.DeviceIdType.MESH
ORDER = (1, 2, 0, 3, 7, 4, 6, 5)
FIRST = (0, 1, 6, 7)
READY = {3: (1, 2), 4: (0, 3), 5: (7, 4, 6, 5)}


def kernel(
    dims,
    inter_ref, res_ref, rec_ref, courant, prev, cur, accel, model,
    nm, adj, born,
    ac, ach, co, ap, ax, mo, p1, p1h, ad, img, v1, s2, w2, part,
    qd, ct, hot, b1, b1h, b2, b2h, wt, exs, exr, own, stv, ar,
    ld, h_s, h_r, p_s, p_r, b_s, b_r, st_s, st_r, z1_s, z1_r, z2_s, z2_r, ex_s, ex_r, ar_s, ar_r,
):
    shots, slabs, depth, wide, width, tiles, tx, nrec = dims
    f32 = jnp.float32
    z = lax.axis_index("shot")
    k = lax.axis_index("slab")
    par = z % 2
    pair_a = z + 1 - 2 * par
    pair_b = shots - 1 - z
    up = (k + 1) % slabs
    down = (k + slabs - 1) % slabs

    core = k % 2
    chip = k // 2
    chips = slabs // 2
    phases = (
        (chips, chip, [(z, (chip + d) % chips * 2 + core) for d in range(1, chips)]),
        (
            2 * shots,
            2 * z + core,
            [((2 * z + core + d) % (2 * shots) // 2, chip * 2 + (core + d) % 2) for d in range(1, 2 * shots)],
        ),
    )
    middle = list(range(2, depth - 2))
    outer = [0, 1, depth - 2, depth - 1]
    parts = (slice(0, depth - 4), slice(depth - 4, depth))
    slots = (list(enumerate(middle)), [(depth - 4 + i, d) for i, d in enumerate(outer)])

    barrier = pltpu.get_barrier_semaphore()
    greet = [(z, up), (z, down)] + [dev for phase in phases for dev in phase[2]]
    for dev in greet:
        pl.semaphore_signal(barrier, inc=1, device_id=dev, device_id_type=MESH)

    def strip(j):
        return slice(j * tx, j * tx + tx)

    def load(src, dst, at):
        copies = [pltpu.make_async_copy(src.at[:, strip(j)], dst.at[j], ld.at[at, j]) for j in range(tiles)]
        for copy in copies:
            copy.start()
        return copies

    l_cur = load(cur.at[0], ac, 0)
    l_co = load(courant.at[0], co, 1)
    l_ap = load(prev.at[0], ap, 2)
    l_a1 = load(accel.at[0, 1], ax.at[1], 3)
    l_a0 = load(accel.at[0, 0], ax.at[0], 4)
    l_a2 = load(accel.at[0, 2], ax.at[2], 5)
    l_mo = pltpu.make_async_copy(model, mo, ld.at[6, 0])
    l_mo.start()

    def wait(copies):
        for copy in copies:
            copy.wait()

    def remote(src, dst, send, recv, dev):
        return pltpu.make_async_remote_copy(
            src_ref=src, dst_ref=dst, send_sem=send, recv_sem=recv, device_id=dev, device_id_type=MESH
        )

    start = inter_ref[0, 0]
    stv[0] = jnp.full(stv.shape[1:], start, jnp.int32)

    rec = rec_ref[...] - k * (depth * wide * width)
    inside = (rec >= 0) & (rec < depth * wide * width)
    line = rec // width
    down_at, along = line // wide, line % wide
    row = jnp.where(inside, (along // tx * depth + down_at) * tx + along % tx, -1)
    col = rec % width
    col_at = lax.broadcasted_iota(jnp.int32, (width, nrec), 0) == col
    for f in range(4):
        rest = jnp.concatenate([res_ref[f, i : i + 1, :] for i in range(nrec // 128)], axis=1) if f < 3 else jnp.ones((1, nrec), f32)
        for piece in range(3 if f < 3 else 1):
            bits = rest.astype(jnp.bfloat16).astype(f32)
            rest = rest - bits
            ct[f, :, piece * nrec : piece * nrec + nrec] = jnp.where(col_at, bits, 0.0).astype(jnp.bfloat16)

    def mark(t, carry):
        at = lax.broadcasted_iota(jnp.int32, (depth * tx, nrec), 0) + t * (depth * tx)
        hot[t] = jnp.where(at == row, 1.0, 0.0).astype(jnp.bfloat16)
        return carry

    lax.fori_loop(0, tiles, mark, 0, unroll=2)

    def receivers(fields):
        def group_of(t, carry):
            lines = jnp.concatenate([hot[4 * t + i] for i in range(4)], axis=0)
            triple = jnp.concatenate([lines] * 3, axis=1)
            for f in fields:
                total = lax.dot_general(
                    triple if f < 3 else lines,
                    ct[f] if f < 3 else ct[f, :, 0:nrec],
                    (((1,), (1,)), ((), ())),
                    preferred_element_type=f32,
                )
                for i in range(4):
                    for d in range(depth):
                        first = (i * depth + d) * tx
                        qd[f, 4 * t + i, d] = total[first : first + tx]
            return carry

        lax.fori_loop(0, tiles // 4, group_of, 0)

    receivers((2, 1))

    pl.semaphore_wait(barrier, len(greet))

    halos_c = []
    for j in range(tiles):
        halos_c.append(remote(cur.at[0, depth - 1, strip(j)], ach.at[0, j], h_s.at[0, j], h_r.at[0, j], (z, up)))
        halos_c.append(remote(cur.at[0, 0, strip(j)], ach.at[1, j], h_s.at[1, j], h_r.at[1, j], (z, down)))
    for copy in halos_c:
        copy.start()
    st_a = remote(stv.at[0], stv.at[1], st_s.at[0], st_r.at[0], (pair_a, k))
    st_b = remote(stv.at[0], stv.at[2], st_s.at[1], st_r.at[1], (pair_b, k))
    st_a.start()
    st_b.start()


    lane = lax.broadcasted_iota(jnp.int32, (tx, width), 1)

    def lap(c, below, above, before, after):
        big = jnp.concatenate([before, c, after], axis=0)
        n = below + above
        n = n + pltpu.roll(big, 1, 0)[8 : tx + 8]
        n = n + pltpu.roll(big, tx + 15, 0)[8 : tx + 8]
        n = n + jnp.where(lane == 0, 0.0, pltpu.roll(c, 1, 1))
        n = n + jnp.where(lane == width - 1, 0.0, pltpu.roll(c, width - 1, 1))
        return n - 6.0 * c

    def cells(field, halos, d, i, j):
        c = field[i, d]
        before = jnp.where(j == 0, 0.0, field[(i + tiles - 1) % tiles, d, tx - 8 : tx])
        after = jnp.where(j == tiles - 1, 0.0, field[(i + 1) % tiles, d, 0:8])
        edge_low = isinstance(d, int) and d == 0
        edge_high = isinstance(d, int) and d == depth - 1
        below = jnp.where(k == 0, 0.0, halos[0, i]) if edge_low else field[i, d - 1]
        above = jnp.where(k == slabs - 1, 0.0, halos[1, i]) if edge_high else field[i, d + 1]
        return c, lap(c, below, above, before, after)

    def planes(body, first, last):
        def plane(d, carry):
            def one(j, inner):
                body(d, j)
                return inner

            return lax.fori_loop(0, tiles, one, carry, unroll=4)

        lax.fori_loop(first, last, plane, 0)

    def p1_cell(d, j):
        c, l = cells(ac, ach, d, j, j)
        p1[j, d] = 2.0 * c - ap[j, d] + co[j, d] * l + qd[2, j, d]

    def p1_sends(j):
        return (
            remote(p1.at[j, depth - 1], p1h.at[0, j], p_s.at[0, j], p_r.at[0, j], (z, up)),
            remote(p1.at[j, 0], p1h.at[1, j], p_s.at[1, j], p_r.at[1, j], (z, down)),
        )

    def ad_cell(d, j):
        c, l = cells(p1, p1h, d, j, j)
        a = 2.0 * c - ac[j, d] + co[j, d] * l + qd[1, j, d]
        ad[j, d] = a
        adj[0, d, pl.ds(pl.multiple_of(j * tx, tx), tx), :] = a

    def place(r):
        return (r - start) & (tiles - 1)

    def send1(r, h):
        dev = (pair_a if r in FIRST else pair_b, k)
        return remote(img.at[r, parts[h]], v1.at[r, parts[h]], z1_s.at[r, h], z1_r.at[r, h], dev)

    def send2(r, h):
        dev = (pair_b if r in FIRST else pair_a, k)
        return remote(s2.at[r, parts[h]], w2.at[r, parts[h]], z2_s.at[r, h], z2_r.at[r, h], dev)

    def images(h):
        for r in ORDER:
            at = place(r)
            for slot, d in slots[h]:
                img[r, slot] = ax[1, at, d] * p1[at, d] + ax[0, at, d] * ad[at, d]
            send1(r, h).start()

    wait(l_cur)
    wait(l_co)
    wait(l_ap)
    planes(p1_cell, 1, depth - 1)
    planes(ad_cell, 2, depth - 2)
    wait(l_a1)
    wait(l_a0)
    wait(l_a2)
    images(0)
    for copy in halos_c:
        copy.wait_recv()

    def p1_edge(j, carry):
        p1_cell(0, j)
        p1_cell(depth - 1, j)
        for copy in p1_sends(j):
            copy.start()
        return carry

    lax.fori_loop(0, tiles, p1_edge, 0)
    planes(ad_cell, 1, 2)
    planes(ad_cell, depth - 2, depth - 1)

    def ad_edge(j, carry):
        for copy in p1_sends(j):
            copy.wait_recv()
        ad_cell(0, j)
        ad_cell(depth - 1, j)
        return carry

    lax.fori_loop(0, tiles, ad_edge, 0)
    images(1)

    receivers((0, 3))
    st_a.wait_recv()
    st_b.wait_recv()

    def group(slot, r):
        cell = jnp.where(stv[slot] > r, 1, 0)
        across = jnp.concatenate([cell] * (width // 128), axis=1)
        return jnp.concatenate([across] * (tx // 8), axis=0)

    for h in range(2):
        for r in ORDER:
            first, second = (1, 2) if r in FIRST else (2, 1)
            send1(r, h).wait_recv()
            g_own, g_src, g_dst = group(0, r), group(first, r), group(second, r)
            own_dst = g_own == g_dst
            src_dst = g_src == g_dst
            src_own = g_src == g_own
            for slot, _ in slots[h]:
                mine = img[r, slot]
                theirs = v1[r, slot]
                s2[r, slot] = jnp.where(own_dst, mine, 0.0) + jnp.where(src_dst, theirs, 0.0)
                part[r, slot] = mine + jnp.where(src_own, theirs, 0.0)
            if h == 1:
                send2(r, 1).start()
    for r in ORDER:
        send2(r, 0).start()

    half = tiles // 2

    def extra(e):
        if e < half // 2:
            dest = (1 - par) * pair_a + par * pair_b
        else:
            dest = par * pair_a + (1 - par) * pair_b
        return remote(exs.at[e], exr.at[e], ex_s.at[e], ex_r.at[e], (dest, k)), dest

    for e in range(half):
        copy, dest = extra(e)
        low = e < half // 2
        r_send = (1 - par) * half + e
        r_own = par * half + e
        src_send = jnp.where((par == 1) if low else (par == 0), group(1, r_send), group(2, r_send))
        src_own = jnp.where((par == 0) if low else (par == 1), group(1, r_own), group(2, r_own))
        want_send = dest // 2
        want_own = z // 2
        m_send = group(0, r_send) == want_send
        t_send = src_send == want_send
        m_own = group(0, r_own) == want_own
        t_own = src_own == want_own

        def spread(d, carry, e=e, r_send=r_send, r_own=r_own, m_send=m_send, t_send=t_send, m_own=m_own, t_own=t_own):
            exs[e, d] = jnp.where(m_send, img[r_send, d], 0.0) + jnp.where(t_send, v1[r_send, d], 0.0)
            own[e, d] = jnp.where(m_own, img[r_own, d], 0.0) + jnp.where(t_own, v1[r_own, d], 0.0)
            return carry

        lax.fori_loop(0, depth, spread, 0, unroll=2)
        copy.start()

    def fold(m):
        m = sum(m[:, 128 * i : 128 * i + 128] for i in range(width // 128))
        return sum(m[8 * i : 8 * i + 8] for i in range(tx // 8))

    def tally(carry, t, d, at, b):
        num, den = carry
        return num + fold(qd[t, at, d] * b), den + fold(qd[3, at, d] * b * b)

    def halo_sends(level, field, halos, r):
        return (
            remote(field.at[r, depth - 1], halos.at[0, r], b_s.at[level, 0, r], b_r.at[level, 0, r], (z, up)),
            remote(field.at[r, 0], halos.at[1, r], b_s.at[level, 1, r], b_r.at[level, 1, r], (z, down)),
        )

    zero = jnp.zeros((8, 128), f32)
    sums = (zero, zero)

    def born1(h, carry):
        for r in ORDER:
            send2(r, h).wait_recv()
            at = place(r)
            for slot, d in slots[h]:
                w = co[at, d] * (part[r, slot] + w2[r, slot])
                wt[r, d] = w
                b = w * ax[0, at, d]
                b1[r, d] = b
                carry = tally(carry, 0, d, at, b)
            if h == 1:
                for copy in halo_sends(0, b1, b1h, r):
                    copy.start()
            elif r in READY:
                carry = b2_tiles(READY[r], carry)
        return carry


    def b2_cell(d, r, carry):
        j = place(r)
        c, l = cells(b1, b1h, d, r, j)
        b = 2.0 * c + co[j, d] * l + wt[r, d] * ax[1, j, d]
        b2[r, d] = b
        return tally(carry, 1, d, j, b)

    def b3_cell(d, j, carry):
        r = (j + start) & (tiles - 1)
        c, l = cells(b2, b2h, d, r, j)
        b = 2.0 * c - b1[r, d] + co[j, d] * l + wt[r, d] * ax[2, j, d]
        born[0, d, pl.ds(pl.multiple_of(j * tx, tx), tx), :] = b
        return tally(carry, 2, d, j, b)

    def sweep(carry):
        def plane(d, inner):
            return lax.fori_loop(0, tiles, lambda j, deep: b3_cell(d, j, deep), inner, unroll=4)

        return lax.fori_loop(1, depth - 1, plane, carry)

    def b2_tiles(chosen, carry):
        def plane(d, inner):
            for r in chosen:
                inner = b2_cell(d, r, inner)
            return inner

        return lax.fori_loop(1, depth - 1, plane, carry)

    def b2_edge(r, carry):
        for copy in halo_sends(0, b1, b1h, r):
            copy.wait_recv()
        carry = b2_cell(0, r, carry)
        carry = b2_cell(depth - 1, r, carry)
        for copy in halo_sends(1, b2, b2h, r):
            copy.start()
        return carry

    sums = born1(1, sums)
    sums = lax.fori_loop(0, tiles, b2_edge, sums)
    for copy in halos_c:
        copy.wait_send()
    st_a.wait_send()
    st_b.wait_send()

    def drain(j, carry):
        for copy in p1_sends(j):
            copy.wait_send()
        for copy in halo_sends(0, b1, b1h, j):
            copy.wait_send()
        for copy in halo_sends(1, b2, b2h, j):
            copy.wait_send()
        return carry

    lax.fori_loop(0, tiles, drain, 0)
    for r in range(tiles):
        send1(r, 0).wait_send()
        send1(r, 1).wait_send()
        send2(r, 1).wait_send()

    sums = born1(0, sums)
    sums = sweep(sums)

    def b2_wait(r, carry):
        for copy in halo_sends(1, b2, b2h, r):
            copy.wait_recv()
        return carry

    lax.fori_loop(0, tiles, b2_wait, 0)

    def b3_edge(j, carry):
        carry = b3_cell(0, j, carry)
        return b3_cell(depth - 1, j, carry)

    sums = lax.fori_loop(0, tiles, b3_edge, sums)

    row_at = lax.broadcasted_iota(jnp.int32, (8, 128), 0)
    num = jnp.sum(sums[0], axis=0, keepdims=True)
    den = jnp.sum(sums[1], axis=0, keepdims=True)
    total = jnp.where(row_at == 0, num, jnp.where(row_at == 1, den, 0.0))
    for at, (n, coord, partners) in enumerate(phases):
        ar[at, coord] = total
        for d, dev in enumerate(partners):
            remote(ar.at[at, coord], ar.at[at, coord], ar_s.at[at, d], ar_r.at[at, coord], dev).start()
        if at == 0:
            for r in range(tiles):
                send2(r, 0).wait_send()
            l_mo.wait()
        for d, dev in enumerate(partners):
            other = (coord + 1 + d) % n
            remote(ar.at[at, other], ar.at[at, other], ar_s.at[at, d], ar_r.at[at, other], dev).wait_recv()
        total = ar[at, 0]
        for slot in range(1, n):
            total = total + ar[at, slot]
    num = jnp.sum(total[0:1], axis=1, keepdims=True)
    den = jnp.sum(total[1:2], axis=1, keepdims=True)
    alpha = num / (den + 1e-6)

    for e in range(half):
        copy = extra(e)[0]
        copy.wait_recv()
        for slot, d in slots[0] + slots[1]:
            cells_at = slice(e * tx, e * tx + tx)
            nm[d, cells_at, :] = mo[d, cells_at, :] - alpha * (own[e, slot] + exr[e, slot])
        copy.wait_send()
    for at, (n, coord, partners) in enumerate(phases):
        for d, dev in enumerate(partners):
            remote(ar.at[at, coord], ar.at[at, coord], ar_s.at[at, d], ar_r.at[at, coord], dev).wait_send()


def local(courant, adj_prev, adj_cur, accel, res_data, rec_index, intersection, model):
    shots, slabs = lax.axis_size("shot"), lax.axis_size("slab")
    depth, wide, width = courant.shape[1:]
    tiles = intersection.shape[1]
    tx = wide // tiles
    nrec = rec_index.shape[1]
    f32 = jnp.float32
    dims = (shots, slabs, depth, wide, width, tiles, tx, nrec)
    tiled = (tiles, depth, tx, width)
    part = (tiles // 2, depth, tx, width)
    most = max(slabs // 2, 2 * shots)
    dma = pltpu.SemaphoreType.DMA
    vm = pltpu.VMEM
    halo = (2, tiles, tx, width)
    scratch = [
        vm(tiled, f32), vm(halo, f32), vm(tiled, f32), vm(tiled, f32), vm((3,) + tiled, f32),
        vm(model.shape, f32), vm(tiled, f32), vm(halo, f32), vm(tiled, f32),
        vm(tiled, f32), vm(tiled, f32), vm(tiled, f32), vm(tiled, f32), vm(tiled, f32),
        vm((4,) + tiled, f32), vm((4, width, 3 * nrec), jnp.bfloat16), vm((tiles, depth * tx, nrec), jnp.bfloat16),
        vm(tiled, f32), vm(halo, f32), vm(tiled, f32), vm(halo, f32),
        vm(tiled, f32), vm(part, f32), vm(part, f32), vm(part, f32),
        vm((3, 8, 128), jnp.int32), vm((2, most, 8, 128), f32),
        dma((7, tiles)), dma((2, tiles)), dma((2, tiles)), dma((2, tiles)), dma((2, tiles)),
        dma((2, 2, tiles)), dma((2, 2, tiles)), dma((2,)), dma((2,)),
        dma((tiles, 2)), dma((tiles, 2)), dma((tiles, 2)), dma((tiles, 2)),
        dma((tiles // 2,)), dma((tiles // 2,)), dma((2, most)), dma((2, most)),
    ]
    any_spec = pl.BlockSpec(memory_space=pl.ANY)
    vm_spec = pl.BlockSpec(memory_space=pltpu.VMEM)
    return pl.pallas_call(
        functools.partial(kernel, dims),
        out_shape=(
            pltpu.VMEM(model.shape, f32),
            pltpu.VMEM(courant.shape, f32),
            pltpu.VMEM(courant.shape, f32),
        ),
        in_specs=[pl.BlockSpec(memory_space=pltpu.SMEM), vm_spec, vm_spec] + [any_spec] * 5,
        out_specs=(vm_spec,) * 3,
        scratch_shapes=scratch,
        compiler_params=pltpu.CompilerParams(
            collective_id=0, has_side_effects=True, vmem_limit_bytes=57 * 1024 * 1024
        ),
    )(intersection, res_data.reshape(3, nrec // 128, 128), rec_index, courant, adj_prev, adj_cur, accel, model)


def solution(mesh):
    in_specs = (
        P("shot", "slab", None, None),
        P("shot", "slab", None, None),
        P("shot", "slab", None, None),
        P("shot", None, "slab", None, None),
        P("shot", None, None),
        P("shot", None),
        P("shot", None),
        P("slab", "shot", None),
    )
    out_specs = (
        P("slab", "shot", None),
        P("shot", "slab", None, None),
        P("shot", "slab", None, None),
    )
    return jax.shard_map(local, mesh=mesh, in_specs=in_specs, out_specs=out_specs, check_vma=False)
```

```python
import functools

import jax
import jax.numpy as jnp
from jax import lax
from jax.experimental import pallas as pl
from jax.experimental.pallas import tpu as pltpu
from jax.sharding import PartitionSpec as P

MESH = pl.DeviceIdType.MESH
ORDER = (1, 2, 0, 3, 7, 4, 6, 5)
FIRST = (0, 1, 6, 7)
READY = {3: (1, 2), 4: (0, 3), 5: (7, 4, 6, 5)}


def kernel(
    dims,
    inter_ref, res_ref, rec_ref, courant, prev, cur, accel, model,
    nm, adj, born,
    ac, ach, co, ap, ax, mo, p1, p1h, ad, img, v1, s2, w2, part,
    qd, ct, hot, b1, b1h, b2, b2h, wt, exs, exr, own, stv, ar,
    ld, h_s, h_r, p_s, p_r, b_s, b_r, st_s, st_r, z1_s, z1_r, z2_s, z2_r, ex_s, ex_r, ar_s, ar_r,
):
    shots, slabs, depth, wide, width, tiles, tx, nrec = dims
    f32 = jnp.float32
    z = lax.axis_index("shot")
    k = lax.axis_index("slab")
    par = z % 2
    pair_a = z + 1 - 2 * par
    pair_b = shots - 1 - z
    up = (k + 1) % slabs
    down = (k + slabs - 1) % slabs

    core = k % 2
    chip = k // 2
    chips = slabs // 2
    phases = (
        (chips, chip, [(z, (chip + d) % chips * 2 + core) for d in range(1, chips)]),
        (
            2 * shots,
            2 * z + core,
            [((2 * z + core + d) % (2 * shots) // 2, chip * 2 + (core + d) % 2) for d in range(1, 2 * shots)],
        ),
    )
    middle = list(range(2, depth - 2))
    outer = [0, 1, depth - 2, depth - 1]
    parts = (slice(0, depth - 4), slice(depth - 4, depth))
    slots = (list(enumerate(middle)), [(depth - 4 + i, d) for i, d in enumerate(outer)])

    barrier = pltpu.get_barrier_semaphore()
    greet = [(z, up), (z, down)] + [dev for phase in phases for dev in phase[2]]
    for dev in greet:
        pl.semaphore_signal(barrier, inc=1, device_id=dev, device_id_type=MESH)

    def load(src, dst, at):
        copy = pltpu.make_async_copy(src, dst, ld.at[at])
        copy.start()
        return copy

    l_cur = load(cur.at[0], ac, 0)
    l_co = load(courant.at[0], co, 1)
    l_ap = load(prev.at[0], ap, 2)
    l_a1 = load(accel.at[0, 1], ax.at[1], 3)
    l_a0 = load(accel.at[0, 0], ax.at[0], 4)
    l_a2 = load(accel.at[0, 2], ax.at[2], 5)
    l_mo = load(model, mo, 6)

    def remote(src, dst, send, recv, dev):
        return pltpu.make_async_remote_copy(
            src_ref=src, dst_ref=dst, send_sem=send, recv_sem=recv, device_id=dev, device_id_type=MESH
        )

    start = inter_ref[0, 0]
    stv[0] = jnp.full(stv.shape[1:], start, jnp.int32)

    rec = rec_ref[...] - k * (depth * wide * width)
    inside = (rec >= 0) & (rec < depth * wide * width)
    line = rec // width
    down_at, along = line // wide, line % wide
    row = jnp.where(inside, (along // tx * depth + down_at) * tx + along % tx, -1)
    col = rec % width
    col_at = lax.broadcasted_iota(jnp.int32, (width, nrec), 0) == col
    for f in range(4):
        rest = jnp.concatenate([res_ref[f, i : i + 1, :] for i in range(nrec // 128)], axis=1) if f < 3 else jnp.ones((1, nrec), f32)
        for piece in range(3 if f < 3 else 1):
            bits = rest.astype(jnp.bfloat16).astype(f32)
            rest = rest - bits
            ct[f, :, piece * nrec : piece * nrec + nrec] = jnp.where(col_at, bits, 0.0).astype(jnp.bfloat16)

    def mark(t, carry):
        at = lax.broadcasted_iota(jnp.int32, (depth * tx, nrec), 0) + t * (depth * tx)
        hot[t] = jnp.where(at == row, 1.0, 0.0).astype(jnp.bfloat16)
        return carry

    lax.fori_loop(0, tiles, mark, 0, unroll=2)

    def receivers(fields):
        def group_of(t, carry):
            lines = jnp.concatenate([hot[4 * t + i] for i in range(4)], axis=0)
            triple = jnp.concatenate([lines] * 3, axis=1)
            for f in fields:
                total = lax.dot_general(
                    triple if f < 3 else lines,
                    ct[f] if f < 3 else ct[f, :, 0:nrec],
                    (((1,), (1,)), ((), ())),
                    preferred_element_type=f32,
                )
                for i in range(4):
                    for d in range(depth):
                        first = (i * depth + d) * tx
                        qd[f, 4 * t + i, d] = total[first : first + tx]
            return carry

        lax.fori_loop(0, tiles // 4, group_of, 0)

    receivers((2, 1))

    pl.semaphore_wait(barrier, len(greet))

    halos_c = [
        remote(cur.at[0, depth - 1], ach.at[0], h_s.at[0], h_r.at[0], (z, up)),
        remote(cur.at[0, 0], ach.at[1], h_s.at[1], h_r.at[1], (z, down)),
    ]
    for copy in halos_c:
        copy.start()
    st_a = remote(stv.at[0], stv.at[1], st_s.at[0], st_r.at[0], (pair_a, k))
    st_b = remote(stv.at[0], stv.at[2], st_s.at[1], st_r.at[1], (pair_b, k))
    st_a.start()
    st_b.start()


    lane = lax.broadcasted_iota(jnp.int32, (tx, width), 1)

    def lap(c, below, above, before, after):
        big = jnp.concatenate([before, c, after], axis=0)
        n = below + above
        n = n + pltpu.roll(big, 1, 0)[8 : tx + 8]
        n = n + pltpu.roll(big, tx + 15, 0)[8 : tx + 8]
        n = n + jnp.where(lane == 0, 0.0, pltpu.roll(c, 1, 1))
        n = n + jnp.where(lane == width - 1, 0.0, pltpu.roll(c, width - 1, 1))
        return n - 6.0 * c

    def cells(field, halos, d, i, j):
        def at(tile, plane):
            return (plane, tile) if field is ac else (tile, plane)

        c = field[at(i, d)]
        before = jnp.where(j == 0, 0.0, field[at((i + tiles - 1) % tiles, d) + (slice(tx - 8, tx),)])
        after = jnp.where(j == tiles - 1, 0.0, field[at((i + 1) % tiles, d) + (slice(0, 8),)])
        edge_low = isinstance(d, int) and d == 0
        edge_high = isinstance(d, int) and d == depth - 1
        below = jnp.where(k == 0, 0.0, halos[0, i]) if edge_low else field[at(i, d - 1)]
        above = jnp.where(k == slabs - 1, 0.0, halos[1, i]) if edge_high else field[at(i, d + 1)]
        return c, lap(c, below, above, before, after)

    def planes(body, first, last):
        def plane(d, carry):
            def one(j, inner):
                body(d, j)
                return inner

            return lax.fori_loop(0, tiles, one, carry, unroll=4)

        lax.fori_loop(first, last, plane, 0)

    def p1_cell(d, j):
        c, l = cells(ac, ach, d, j, j)
        p1[j, d] = 2.0 * c - ap[d, j] + co[d, j] * l + qd[2, j, d]

    def p1_sends(j):
        return (
            remote(p1.at[j, depth - 1], p1h.at[0, j], p_s.at[0, j], p_r.at[0, j], (z, up)),
            remote(p1.at[j, 0], p1h.at[1, j], p_s.at[1, j], p_r.at[1, j], (z, down)),
        )

    def place(r):
        return (r - start) & (tiles - 1)

    def send1(r, h):
        dev = (pair_a if r in FIRST else pair_b, k)
        return remote(img.at[r, parts[h]], v1.at[r, parts[h]], z1_s.at[r, h], z1_r.at[r, h], dev)

    def send2(r, h):
        dev = (pair_b if r in FIRST else pair_a, k)
        return remote(s2.at[r, parts[h]], w2.at[r, parts[h]], z2_s.at[r, h], z2_r.at[r, h], dev)

    def images(h):
        for r in ORDER:
            at = place(r)
            for slot, d in slots[h]:
                c, l = cells(p1, p1h, d, at, at)
                a = 2.0 * c - ac[d, at] + co[d, at] * l + qd[1, at, d]
                ad[r, d] = a
                img[r, slot] = ax[1, d, at] * c + ax[0, d, at] * a
            send1(r, h).start()

    l_cur.wait()
    l_co.wait()
    l_ap.wait()
    planes(p1_cell, 1, depth - 1)
    l_a1.wait()
    l_a0.wait()
    l_a2.wait()
    images(0)
    for copy in halos_c:
        copy.wait_recv()

    def p1_edge(j, carry):
        p1_cell(0, j)
        p1_cell(depth - 1, j)
        for copy in p1_sends(j):
            copy.start()
        return carry

    lax.fori_loop(0, tiles, p1_edge, 0)

    def p1_wait(j, carry):
        for copy in p1_sends(j):
            copy.wait_recv()
        return carry

    lax.fori_loop(0, tiles, p1_wait, 0)
    images(1)

    def ad_out(d, carry):
        for j in range(tiles):
            adj[0, d, j] = ad[(j + start) & (tiles - 1), d]
        return carry

    lax.fori_loop(0, depth, ad_out, 0)

    receivers((0, 3))
    st_a.wait_recv()
    st_b.wait_recv()

    def group(slot, r):
        cell = jnp.where(stv[slot] > r, 1, 0)
        across = jnp.concatenate([cell] * (width // 128), axis=1)
        return jnp.concatenate([across] * (tx // 8), axis=0)

    for h in range(2):
        for r in ORDER:
            first, second = (1, 2) if r in FIRST else (2, 1)
            send1(r, h).wait_recv()
            g_own, g_src, g_dst = group(0, r), group(first, r), group(second, r)
            own_dst = g_own == g_dst
            src_dst = g_src == g_dst
            src_own = g_src == g_own
            for slot, _ in slots[h]:
                mine = img[r, slot]
                theirs = v1[r, slot]
                s2[r, slot] = jnp.where(own_dst, mine, 0.0) + jnp.where(src_dst, theirs, 0.0)
                part[r, slot] = mine + jnp.where(src_own, theirs, 0.0)
            if h == 1:
                send2(r, 1).start()
    for r in ORDER:
        send2(r, 0).start()

    half = tiles // 2

    def extra(e):
        if e < half // 2:
            dest = (1 - par) * pair_a + par * pair_b
        else:
            dest = par * pair_a + (1 - par) * pair_b
        return remote(exs.at[e], exr.at[e], ex_s.at[e], ex_r.at[e], (dest, k)), dest

    for e in range(half):
        copy, dest = extra(e)
        low = e < half // 2
        r_send = (1 - par) * half + e
        r_own = par * half + e
        src_send = jnp.where((par == 1) if low else (par == 0), group(1, r_send), group(2, r_send))
        src_own = jnp.where((par == 0) if low else (par == 1), group(1, r_own), group(2, r_own))
        want_send = dest // 2
        want_own = z // 2
        m_send = group(0, r_send) == want_send
        t_send = src_send == want_send
        m_own = group(0, r_own) == want_own
        t_own = src_own == want_own

        def spread(d, carry, e=e, r_send=r_send, r_own=r_own, m_send=m_send, t_send=t_send, m_own=m_own, t_own=t_own):
            exs[e, d] = jnp.where(m_send, img[r_send, d], 0.0) + jnp.where(t_send, v1[r_send, d], 0.0)
            own[e, d] = jnp.where(m_own, img[r_own, d], 0.0) + jnp.where(t_own, v1[r_own, d], 0.0)
            return carry

        lax.fori_loop(0, depth, spread, 0, unroll=2)
        copy.start()

    def fold(m):
        m = sum(m[:, 128 * i : 128 * i + 128] for i in range(width // 128))
        return sum(m[8 * i : 8 * i + 8] for i in range(tx // 8))

    def tally(carry, t, d, at, b):
        num, den = carry
        return num + fold(qd[t, at, d] * b), den + fold(qd[3, at, d] * b * b)

    def halo_sends(level, field, halos, r):
        return (
            remote(field.at[r, depth - 1], halos.at[0, r], b_s.at[level, 0, r], b_r.at[level, 0, r], (z, up)),
            remote(field.at[r, 0], halos.at[1, r], b_s.at[level, 1, r], b_r.at[level, 1, r], (z, down)),
        )

    zero = jnp.zeros((8, 128), f32)
    sums = (zero, zero)

    def born1(h, carry):
        for r in ORDER:
            send2(r, h).wait_recv()
            at = place(r)
            for slot, d in slots[h]:
                w = co[d, at] * (part[r, slot] + w2[r, slot])
                wt[r, d] = w
                b = w * ax[0, d, at]
                b1[r, d] = b
                carry = tally(carry, 0, d, at, b)
            if h == 1:
                for copy in halo_sends(0, b1, b1h, r):
                    copy.start()
            elif r in READY:
                carry = b2_tiles(READY[r], carry)
        return carry


    def b2_cell(d, r, carry):
        j = place(r)
        c, l = cells(b1, b1h, d, r, j)
        b = 2.0 * c + co[d, j] * l + wt[r, d] * ax[1, d, j]
        b2[r, d] = b
        return tally(carry, 1, d, j, b)

    def b3_cell(d, j, carry):
        r = (j + start) & (tiles - 1)
        c, l = cells(b2, b2h, d, r, j)
        b = 2.0 * c - b1[r, d] + co[d, j] * l + wt[r, d] * ax[2, d, j]
        born[0, d, j] = b
        return tally(carry, 2, d, j, b)

    def sweep(carry):
        def plane(d, inner):
            return lax.fori_loop(0, tiles, lambda j, deep: b3_cell(d, j, deep), inner, unroll=4)

        return lax.fori_loop(1, depth - 1, plane, carry)

    def b2_tiles(chosen, carry):
        def plane(d, inner):
            for r in chosen:
                inner = b2_cell(d, r, inner)
            return inner

        return lax.fori_loop(1, depth - 1, plane, carry)

    def b2_edge(r, carry):
        for copy in halo_sends(0, b1, b1h, r):
            copy.wait_recv()
        carry = b2_cell(0, r, carry)
        carry = b2_cell(depth - 1, r, carry)
        for copy in halo_sends(1, b2, b2h, r):
            copy.start()
        return carry

    sums = born1(1, sums)
    sums = lax.fori_loop(0, tiles, b2_edge, sums)
    for copy in halos_c:
        copy.wait_send()
    st_a.wait_send()
    st_b.wait_send()

    def drain(j, carry):
        for copy in p1_sends(j):
            copy.wait_send()
        for copy in halo_sends(0, b1, b1h, j):
            copy.wait_send()
        for copy in halo_sends(1, b2, b2h, j):
            copy.wait_send()
        return carry

    lax.fori_loop(0, tiles, drain, 0)
    for r in range(tiles):
        send1(r, 0).wait_send()
        send1(r, 1).wait_send()
        send2(r, 1).wait_send()

    sums = born1(0, sums)
    sums = sweep(sums)

    def b2_wait(r, carry):
        for copy in halo_sends(1, b2, b2h, r):
            copy.wait_recv()
        return carry

    lax.fori_loop(0, tiles, b2_wait, 0)

    def b3_edge(j, carry):
        carry = b3_cell(0, j, carry)
        return b3_cell(depth - 1, j, carry)

    sums = lax.fori_loop(0, tiles, b3_edge, sums)

    row_at = lax.broadcasted_iota(jnp.int32, (8, 128), 0)
    num = jnp.sum(sums[0], axis=0, keepdims=True)
    den = jnp.sum(sums[1], axis=0, keepdims=True)
    total = jnp.where(row_at == 0, num, jnp.where(row_at == 1, den, 0.0))
    for at, (n, coord, partners) in enumerate(phases):
        ar[at, coord] = total
        for d, dev in enumerate(partners):
            remote(ar.at[at, coord], ar.at[at, coord], ar_s.at[at, d], ar_r.at[at, coord], dev).start()
        if at == 0:
            for r in range(tiles):
                send2(r, 0).wait_send()
            l_mo.wait()
        for d, dev in enumerate(partners):
            other = (coord + 1 + d) % n
            remote(ar.at[at, other], ar.at[at, other], ar_s.at[at, d], ar_r.at[at, other], dev).wait_recv()
        total = ar[at, 0]
        for slot in range(1, n):
            total = total + ar[at, slot]
    num = jnp.sum(total[0:1], axis=1, keepdims=True)
    den = jnp.sum(total[1:2], axis=1, keepdims=True)
    alpha = num / (den + 1e-6)

    for e in range(half):
        copy = extra(e)[0]
        copy.wait_recv()
        for slot, d in slots[0] + slots[1]:
            cells_at = slice(e * tx, e * tx + tx)
            nm[d, cells_at, :] = mo[d, cells_at, :] - alpha * (own[e, slot] + exr[e, slot])
        copy.wait_send()
    for at, (n, coord, partners) in enumerate(phases):
        for d, dev in enumerate(partners):
            remote(ar.at[at, coord], ar.at[at, coord], ar_s.at[at, d], ar_r.at[at, coord], dev).wait_send()


def local(courant, adj_prev, adj_cur, accel, res_data, rec_index, intersection, model):
    shots, slabs = lax.axis_size("shot"), lax.axis_size("slab")
    depth, wide, width = courant.shape[1:]
    tiles = intersection.shape[1]
    tx = wide // tiles
    nrec = rec_index.shape[1]
    f32 = jnp.float32
    dims = (shots, slabs, depth, wide, width, tiles, tx, nrec)
    tiled = (tiles, depth, tx, width)
    part = (tiles // 2, depth, tx, width)
    most = max(slabs // 2, 2 * shots)
    dma = pltpu.SemaphoreType.DMA
    vm = pltpu.VMEM
    halo = (2, tiles, tx, width)
    laid = (depth, tiles, tx, width)
    scratch = [
        vm(laid, f32), vm(halo, f32), vm(laid, f32), vm(laid, f32), vm((3,) + laid, f32),
        vm(model.shape, f32), vm(tiled, f32), vm(halo, f32), vm(tiled, f32),
        vm(tiled, f32), vm(tiled, f32), vm(tiled, f32), vm(tiled, f32), vm(tiled, f32),
        vm((4,) + tiled, f32), vm((4, width, 3 * nrec), jnp.bfloat16), vm((tiles, depth * tx, nrec), jnp.bfloat16),
        vm(tiled, f32), vm(halo, f32), vm(tiled, f32), vm(halo, f32),
        vm(tiled, f32), vm(part, f32), vm(part, f32), vm(part, f32),
        vm((3, 8, 128), jnp.int32), vm((2, most, 8, 128), f32),
        dma((7,)), dma((2,)), dma((2,)), dma((2, tiles)), dma((2, tiles)),
        dma((2, 2, tiles)), dma((2, 2, tiles)), dma((2,)), dma((2,)),
        dma((tiles, 2)), dma((tiles, 2)), dma((tiles, 2)), dma((tiles, 2)),
        dma((tiles // 2,)), dma((tiles // 2,)), dma((2, most)), dma((2, most)),
    ]
    any_spec = pl.BlockSpec(memory_space=pl.ANY)
    vm_spec = pl.BlockSpec(memory_space=pltpu.VMEM)
    new_model, adj, born = pl.pallas_call(
        functools.partial(kernel, dims),
        out_shape=(
            pltpu.VMEM(model.shape, f32),
            pltpu.VMEM((1,) + laid, f32),
            pltpu.VMEM((1,) + laid, f32),
        ),
        in_specs=[pl.BlockSpec(memory_space=pltpu.SMEM), vm_spec, vm_spec] + [any_spec] * 5,
        out_specs=(vm_spec,) * 3,
        scratch_shapes=scratch,
        compiler_params=pltpu.CompilerParams(
            collective_id=0, has_side_effects=True, vmem_limit_bytes=57 * 1024 * 1024
        ),
    )(
        intersection, res_data.reshape(3, nrec // 128, 128), rec_index, courant.reshape((1,) + laid),
        adj_prev.reshape((1,) + laid), adj_cur.reshape((1,) + laid), accel.reshape((1, 3) + laid), model,
    )
    return new_model, adj.reshape(courant.shape), born.reshape(courant.shape)


def solution(mesh):
    in_specs = (
        P("shot", "slab", None, None),
        P("shot", "slab", None, None),
        P("shot", "slab", None, None),
        P("shot", None, "slab", None, None),
        P("shot", None, None),
        P("shot", None),
        P("shot", None),
        P("slab", "shot", None),
    )
    out_specs = (
        P("slab", "shot", None),
        P("shot", "slab", None, None),
        P("shot", "slab", None, None),
    )
    return jax.shard_map(local, mesh=mesh, in_specs=in_specs, out_specs=out_specs, check_vma=False)
```
